512 devices in a mesh: grp: 4 (over x), ep: 128 (over z, y, core).
Axes of the slice: x: 4, y: 8, z: 8, core: 2. Of those that a mesh axis runs over, the one named last changes fastest.
Arguments:
- tokens: bfloat16 [65536, 1024], P(('grp', 'ep')), may hold values from -6 to 6
- routes: int32 [65536, 1], P(('grp', 'ep')), may hold values from 0 to 127; in each aligned block of 128 rows (0 to 127, 128 to 255, ...) at most 2 rows name the same one
- gate_prob: float32 [65536], P(('grp', 'ep')), may hold values from 0.1 to 1
- coef_weight: bfloat16 [1024], replicated, may hold values from -0.1875 to 0.1875
- exp_up: bfloat16 [128, 1024, 4096], P('ep', None, 'grp'), may hold values from -0.1875 to 0.1875
- exp_down: bfloat16 [128, 4096, 1024], P('ep', 'grp'), may hold values from -0.09375 to 0.09375
- res_up: bfloat16 [1024, 4096], P('ep', 'grp'), may hold values from -0.1875 to 0.1875
- res_down: bfloat16 [4096, 1024], P('grp', 'ep'), may hold values from -0.09375 to 0.09375
Outputs:
- mixed: bfloat16 [65536, 1024], P(('grp', 'ep'))
The draws below stay inside these ranges and needn't reach their ends.
Inputs may be any that keep to these rules, and one draw needn't show every extreme that they name: `routes`: rows are taken in aligned blocks of 128, the rows of one device in the order grp then ep. In every block at most 2 rows name the same expert, and some block reaches 2.
All inputs are finite; a program needn't handle non-finite values.
Results may differ from the reference program's by a relative error of at most 0.015.
Values may be sent and summed in bfloat16 or wider, within the bound.
No kernel may reach another device: no remote copies, remote signals or barrier semaphores. Data moves between devices by JAX's collectives and lax.ppermute only.
A program may use at most 64 MiB of HBM per device.

```python
import math
import jax
import jax.numpy as jnp
import numpy as np
from jax import lax

D = 1024
FF_EXP = 4096
FF_RES = 4096
TOK_DEV = 128
EXPERTS = 128
CAP = 2
TOKENS = 65536
N_GRP = 4
N_EP = 128


def shard_levels(own_key, extent, shards, smallest, largest):
    def one(dim, blocks):
        steps = jax.random.uniform(jax.random.fold_in(jax.random.fold_in(own_key, 6), dim), (blocks,), jnp.float32, smallest / len(shards), largest / len(shards))
        return jnp.repeat(jnp.exp(steps), extent[dim] // blocks).reshape((-1,) + (1,) * (len(extent) - dim - 1))

    loudness = one(*shards[0])
    for cut in shards[1:]:
        loudness = loudness * one(*cut)
    return loudness


def deal_out(rng, own, number, rows, amount, top, limit, skew):
    order = jax.random.permutation(rng, amount)
    crowded, usual = portions_of(amount, rows * top, limit, skew, True), portions_of(amount, rows * top, limit, skew, False)
    places = jnp.arange(amount)

    def named(sizes, offset_by):
        used = int((sizes > 0).sum())
        fixed = max(1, used // 4)
        passed = fixed + (places - fixed + offset_by * (used - fixed)) % max(1, amount - fixed)
        return jnp.zeros((amount,), jnp.int32).at[order[jnp.where(places < fixed, places, passed)]].set(jnp.asarray(sizes, jnp.int32))

    sizes = jnp.where(number % 4 == 0, named(crowded, number // 4), named(usual, number - number // 4 - 1))
    mixed = jax.random.permutation(jax.random.fold_in(own, 3), amount)
    giver, taker = mixed[0:amount // 2 * 2:2], mixed[1:amount // 2 * 2:2]
    margin = jnp.minimum(sizes[giver] - 1, limit - sizes[taker]) // 2
    margin = jnp.where((giver == order[0]) | (taker == order[0]) | (sizes[taker] == 0), 0, jnp.maximum(margin, 0))
    passed = jax.random.randint(jax.random.fold_in(own, 4), (amount // 2,), 0, 1 << 20) % (margin + 1)
    sizes = sizes.at[giver].add(-passed).at[taker].add(passed)
    items = jnp.searchsorted(jnp.cumsum(sizes), jnp.arange(rows * top), side="right").astype(jnp.int32)
    grid = items.reshape(top, rows).T
    grid = grid[jax.random.permutation(jax.random.fold_in(own, 1), rows)]
    offset_by = jax.random.randint(jax.random.fold_in(own, 2), (rows, 1), 0, top)
    return jnp.take_along_axis(grid, (jnp.arange(top)[None, :] + offset_by) % top, axis=1)


def portions_of(count, total, reach, skew, full):
    loads = [(1 << 20) // math.isqrt(grade ** skew) + 1 for grade in range(1, count + 1)]
    largest = reach if full else min(reach, max(-(-total // count), total * loads[0] // sum(loads)))
    least = 1 if total - largest >= count - 1 else 0
    counts, rest = [largest] + [least] * (count - 1), total - largest - least * (count - 1)
    while rest > 0:
        candidates = [i for i in range(1, count) if counts[i] < largest] or [i for i in range(1, count) if counts[i] < reach]
        whole, remaining = sum([loads[i] for i in candidates]), rest
        for i in candidates:
            addition = min(reach - counts[i], max(1, remaining * loads[i] // whole), rest)
            counts[i] = counts[i] + addition
            rest = rest - addition
    return np.array(counts)


def bell_draw(rng, shape, spread, reach, shards=(), kind=jnp.bfloat16):
    values = spread * jax.random.normal(rng, shape, jnp.float32)
    if shards:
        values = values * shard_levels(rng, shape, shards, -0.22, 0.18)
    return jnp.clip(values, -reach, reach).astype(kind)


def setup_inputs(seed: int = 0) -> dict:
    splits = jax.random.split(jax.random.key(seed), 9)
    tokens = bell_draw(splits[0], (TOKENS, D), 1.0, 6.0, ((0, 512),))
    routes_keys = jax.random.split(jax.random.fold_in(splits[1], 1), TOKENS // TOK_DEV)
    routes_turns = jax.random.permutation(jax.random.fold_in(splits[1], 3), TOKENS // TOK_DEV)
    routes = jax.vmap(lambda own, number: deal_out(jax.random.fold_in(splits[1], 2), own, number, TOK_DEV, EXPERTS, 1, CAP, 2))(routes_keys, routes_turns).reshape((TOKENS, 1))
    gate_prob = jnp.clip(jnp.exp(math.log(1.0) - 2.3025851 * jax.random.uniform(splits[2], (TOKENS,), jnp.float32) ** shard_levels(splits[2], (TOKENS,), ((0, 512),), -0.2, 0.2)), 0.1, 1.0)
    coef_weight = bell_draw(splits[3], (D,), D ** -0.5, 0.1875)
    exp_up = bell_draw(splits[4], (EXPERTS, D, FF_EXP), D ** -0.5, 0.1875, ((0, 128), (2, 4)))
    exp_down = bell_draw(splits[5], (EXPERTS, FF_EXP, D), FF_EXP ** -0.5, 0.09375, ((0, 128), (1, 4)))
    res_up = bell_draw(splits[6], (D, FF_RES), D ** -0.5, 0.1875, ((0, 128), (1, 4)))
    res_down = bell_draw(splits[7], (FF_RES, D), FF_RES ** -0.5, 0.09375, ((0, 4), (1, 128)))
    return {"tokens": tokens, "routes": routes, "gate_prob": gate_prob, "coef_weight": coef_weight, "exp_up": exp_up, "exp_down": exp_down, "res_up": res_up, "res_down": res_down}


def gelu_hidden(inputs, weight_in):
    product = jnp.dot(inputs, weight_in, preferred_element_type=jnp.float32)
    return jax.nn.gelu(product, approximate=True).astype(jnp.bfloat16)


def block_sum(hidden, weight_out, parts_count):
    row_count = hidden.shape[0]
    part_width = hidden.shape[1] // parts_count
    pieces = hidden.reshape(row_count, parts_count, part_width).astype(jnp.float32)
    blocked = weight_out.reshape(parts_count, part_width, weight_out.shape[1]).astype(jnp.float32)
    partial_value = jnp.einsum("rqf,qfd->rqd", pieces, blocked).astype(jnp.bfloat16)
    partial_value = lax.optimization_barrier(partial_value)
    return jnp.sum(partial_value.astype(jnp.float32), axis=1)


def slot_table(route_row):
    expert_ids = jnp.arange(EXPERTS, dtype=jnp.int32)
    onehot = (route_row[:, None] == expert_ids[None, :]).astype(jnp.int32)
    earlier = jnp.cumsum(onehot, axis=0, dtype=jnp.int32) - onehot
    position = jnp.sum(earlier * onehot, axis=1, dtype=jnp.int32)
    slot_index = route_row * CAP + position
    slot_ids = jnp.arange(EXPERTS * CAP, dtype=jnp.int32)
    return (slot_index[:, None] == slot_ids[None, :]).astype(jnp.bfloat16)


def reference(tokens, routes, gate_prob, coef_weight, exp_up, exp_down, res_up, res_down):
    block_count = N_GRP * N_EP
    route_rows = routes.reshape(block_count, TOK_DEV)
    token_blocks = tokens.reshape(block_count, TOK_DEV, D)
    tables = lax.map(slot_table, route_rows)

    def fill_slots(pair):
        table, block_rows = pair
        return lax.dot_general(table, block_rows, (((0,), (0,)), ((), ())), preferred_element_type=jnp.float32).astype(jnp.bfloat16)

    sent = lax.map(fill_slots, (tables, token_blocks))
    by_expert = jnp.transpose(sent.reshape(block_count, EXPERTS, CAP, D), (1, 0, 2, 3)).reshape(EXPERTS, block_count * CAP, D)

    def serve(triple):
        slot_rows, weight_in, weight_out = triple
        return block_sum(gelu_hidden(slot_rows, weight_in), weight_out, N_GRP).astype(jnp.bfloat16)

    served = lax.map(serve, (by_expert, exp_up, exp_down))
    returned = jnp.transpose(served.reshape(EXPERTS, block_count, CAP, D), (1, 0, 2, 3)).reshape(block_count, EXPERTS * CAP, D)

    def combine(pair):
        table, slot_rows = pair
        return jnp.dot(table, slot_rows, preferred_element_type=jnp.float32)

    expert_out = lax.map(combine, (tables, returned)).reshape(TOKENS, D)

    def residual_branch(block_rows):
        return block_sum(gelu_hidden(block_rows, res_up), res_down, N_GRP)

    res_out = lax.map(residual_branch, tokens.reshape(N_EP, N_GRP * TOK_DEV, D)).reshape(TOKENS, D)
    coef = jax.nn.sigmoid(jnp.dot(tokens, coef_weight, preferred_element_type=jnp.float32))
    mixed = coef[:, None] * res_out + (1.0 - coef[:, None]) * gate_prob[:, None] * expert_out
    return mixed.astype(jnp.bfloat16)
```

```python
import jax
import jax.numpy as jnp
from jax import lax
from jax.sharding import PartitionSpec as P


def two_products(rows, weight_in, weight_out, out_dims):
    product = jnp.dot(rows, weight_in, preferred_element_type=jnp.float32)
    hidden = jax.nn.gelu(product, approximate=True).astype(jnp.bfloat16)
    part = lax.dot_general(
        hidden, weight_out, (((1,), (out_dims,)), ((), ())), preferred_element_type=jnp.float32
    )
    return part.astype(jnp.bfloat16)


def slot_of(route_row, capacity):
    place = jnp.arange(route_row.shape[0], dtype=jnp.int32)
    same = (route_row[:, None] == route_row[None, :]) & (place[None, :] < place[:, None])
    return route_row * capacity + jnp.sum(same.astype(jnp.int32), axis=1)


def shifted(value, step, size):
    return lax.ppermute(value, "grp", [(i, (i + step) % size) for i in range(size)])


def local(tokens, routes, gate_prob, coef_weight, exp_up, exp_down, res_up, res_down):
    row_count, model_width = tokens.shape
    groups = lax.axis_size("grp")
    experts = lax.axis_size("ep")
    capacity = 2 * row_count // experts
    slots = experts * capacity

    res_pair = jnp.concatenate([res_up, res_down.T], axis=1)
    res_all = lax.all_gather(res_pair, "ep", axis=0, tiled=True)
    res_up_all = res_all[:, : res_up.shape[1]]
    res_down_all = res_all[:, res_up.shape[1] :]
    whole_rows = lax.all_gather(tokens, "grp", axis=0, tiled=True)

    slot_index = slot_of(routes[:, 0], capacity)
    table = (slot_index[:, None] == jnp.arange(slots, dtype=jnp.int32)[None, :]).astype(jnp.bfloat16)
    outgoing = lax.dot_general(
        table, tokens, (((0,), (0,)), ((), ())), preferred_element_type=jnp.float32
    ).astype(jnp.bfloat16)
    arrived = lax.all_to_all(
        outgoing.reshape(experts, capacity, model_width), "ep", split_axis=0, concat_axis=0, tiled=True
    ).reshape(slots, model_width)

    steps = [1, groups - 1, 2]
    from_others = [shifted(arrived, step, groups) for step in steps]
    own = lax.optimization_barrier(two_products(arrived, exp_up[0], exp_down[0], 0))
    back = [
        shifted(two_products(rows, exp_up[0], exp_down[0], 0), groups - step, groups)
        for rows, step in zip(from_others, steps)
    ]
    total = own.astype(jnp.float32)
    for part in back:
        total = total + part.astype(jnp.float32)
    returned = lax.all_to_all(
        total.astype(jnp.bfloat16).reshape(experts, capacity, model_width),
        "ep",
        split_axis=0,
        concat_axis=0,
        tiled=True,
    ).reshape(slots, model_width)

    part_res = two_products(whole_rows, res_up_all, res_down_all, 1)
    res_out = lax.psum_scatter(part_res, "grp", scatter_dimension=0, tiled=True).astype(jnp.float32)

    expert_out = jnp.dot(table, returned, preferred_element_type=jnp.float32)
    coef = jax.nn.sigmoid(jnp.dot(tokens, coef_weight, preferred_element_type=jnp.float32))
    mixed = coef[:, None] * res_out + (1.0 - coef[:, None]) * gate_prob[:, None] * expert_out
    return mixed.astype(jnp.bfloat16)


def solution(mesh):
    in_specs = (
        P(("grp", "ep"), None),
        P(("grp", "ep"), None),
        P(("grp", "ep")),
        P(),
        P("ep", None, "grp"),
        P("ep", "grp", None),
        P("ep", "grp"),
        P("grp", "ep"),
    )
    out_specs = P(("grp", "ep"), None)
    return jax.shard_map(local, mesh=mesh, in_specs=in_specs, out_specs=out_specs, check_vma=False)
```

```python
import jax
import jax.numpy as jnp
from jax import lax
from jax.sharding import PartitionSpec as P


def gelu_product(rows, weight_in):
    product = jnp.dot(rows, weight_in, preferred_element_type=jnp.float32)
    return jax.nn.gelu(product, approximate=True).astype(jnp.bfloat16)


def two_products(rows, weight_in, weight_out, out_dim):
    part = lax.dot_general(
        gelu_product(rows, weight_in),
        weight_out,
        (((1,), (out_dim,)), ((), ())),
        preferred_element_type=jnp.float32,
    )
    return part.astype(jnp.bfloat16)


def slot_of(route_row, capacity):
    place = jnp.arange(route_row.shape[0], dtype=jnp.int32)
    same = (route_row[:, None] == route_row[None, :]) & (place[None, :] < place[:, None])
    return route_row * capacity + jnp.sum(same.astype(jnp.int32), axis=1)


def shifted(value, step):
    size = lax.axis_size("grp")
    return lax.ppermute(value, "grp", [(i, (i + step) % size) for i in range(size)])


def exchanged(rows, capacity):
    experts = lax.axis_size("ep")
    cut = rows.reshape(experts, capacity, rows.shape[1])
    return lax.all_to_all(cut, "ep", split_axis=0, concat_axis=0, tiled=True).reshape(rows.shape)


def after(value, earlier):
    return lax.optimization_barrier((value, earlier))[0]


def summed(own, others):
    total = own.astype(jnp.float32)
    for part in others:
        total = total + part.astype(jnp.float32)
    return total


def local(tokens, routes, gate_prob, coef_weight, exp_up, exp_down, res_up, res_down):
    row_count, model_width = tokens.shape
    groups = lax.axis_size("grp")
    experts = lax.axis_size("ep")
    capacity = 2 * row_count // experts
    slots = experts * capacity
    steps = [1, groups - 1, 2]

    res_pair = jnp.concatenate([res_up, res_down.T], axis=1)
    res_all = lax.all_gather(res_pair, "ep", axis=0, tiled=True)
    res_up_all = res_all[:, : res_up.shape[1]]
    res_down_all = res_all[:, res_up.shape[1] :]

    slot_index = slot_of(routes[:, 0], capacity)
    table = (slot_index[:, None] == jnp.arange(slots, dtype=jnp.int32)[None, :]).astype(jnp.bfloat16)
    outgoing = lax.dot_general(
        table, tokens, (((0,), (0,)), ((), ())), preferred_element_type=jnp.float32
    ).astype(jnp.bfloat16)
    arrived = exchanged(outgoing, capacity)
    other_tokens = [shifted(tokens, step) for step in steps]
    arrived = after(arrived, other_tokens)

    from_others = [shifted(arrived, step) for step in steps]
    own = lax.optimization_barrier(two_products(arrived, exp_up[0], exp_down[0], 0))
    parts = [two_products(rows, exp_up[0], exp_down[0], 0) for rows in from_others]
    back = [shifted(part, groups - step) for part, step in zip(parts, steps)]
    total = summed(own, back).astype(jnp.bfloat16)
    returned = exchanged(total, capacity)

    whole_rows = jnp.concatenate([tokens] + other_tokens, axis=0)
    part_res = two_products(after(whole_rows, total), res_up_all, res_down_all, 1)
    pieces = [part_res[i * row_count : (i + 1) * row_count] for i in range(groups)]
    res_back = [shifted(piece, groups - step) for piece, step in zip(pieces[1:], steps)]
    res_out = summed(pieces[0], res_back)

    expert_out = jnp.dot(table, returned, preferred_element_type=jnp.float32)
    coef = jax.nn.sigmoid(jnp.dot(tokens, coef_weight, preferred_element_type=jnp.float32))
    mixed = coef[:, None] * res_out + (1.0 - coef[:, None]) * gate_prob[:, None] * expert_out
    return mixed.astype(jnp.bfloat16)


def solution(mesh):
    in_specs = (
        P(("grp", "ep"), None),
        P(("grp", "ep"), None),
        P(("grp", "ep")),
        P(),
        P("ep", None, "grp"),
        P("ep", "grp", None),
        P("ep", "grp"),
        P("grp", "ep"),
    )
    out_specs = P(("grp", "ep"), None)
    return jax.shard_map(local, mesh=mesh, in_specs=in_specs, out_specs=out_specs, check_vma=False)
```

```python
import functools

import jax
import jax.numpy as jnp
from jax import lax
from jax.experimental import pallas as pl
from jax.experimental.pallas import tpu as pltpu
from jax.sharding import PartitionSpec as P

SMEM = pl.BlockSpec(memory_space=pltpu.SMEM)
PARAMS = pltpu.CompilerParams(vmem_limit_bytes=48 * 1024 * 1024)
WHOLE = pltpu.CompilerParams(vmem_limit_bytes=60 * 1024 * 1024)


def cost(rows, model, hidden):
    return pl.CostEstimate(
        flops=4 * rows * model * hidden,
        bytes_accessed=4 * model * (hidden + rows),
        transcendentals=rows * hidden,
    )


def slot_table(route_row, capacity, slots):
    count = route_row.shape[1]
    route = jnp.broadcast_to(route_row, (count, count))
    earlier = lax.broadcasted_iota(jnp.int32, (count, count), 0) < lax.broadcasted_iota(jnp.int32, (count, count), 1)
    place = jnp.sum(jnp.where((route == jnp.transpose(route)) & earlier, 1, 0), axis=0, keepdims=True)
    slot = jnp.broadcast_to(route_row * capacity + place, (slots, count))
    return jnp.where(lax.broadcasted_iota(jnp.int32, (slots, count), 0) == slot, 1.0, 0.0).astype(jnp.bfloat16)


def dispatch_kernel(routes, tokens, out):
    experts, capacity, model = out.shape
    table = slot_table(routes[...], capacity, experts * capacity)
    rows = jnp.dot(table, tokens[...], preferred_element_type=jnp.float32).astype(jnp.bfloat16)
    out[...] = rows.reshape(experts, capacity, model)


def unpack_kernel(slots, out):
    out[...] = slots[...].reshape(out.shape)


def products(rows, weight_in, weight_out, out_dim):
    product = jnp.dot(rows, weight_in, preferred_element_type=jnp.float32)
    hidden = jax.nn.gelu(product, approximate=True).astype(jnp.bfloat16)
    part = lax.dot_general(
        hidden, weight_out, (((1,), (out_dim,)), ((), ())), preferred_element_type=jnp.float32
    )
    return part.astype(jnp.bfloat16)


def expert_kernel(rows, weight_in, weight_out, out):
    out[...] = products(rows[...], weight_in[0], weight_out[0], 0)


def expert_pair_kernel(left, right, weight_in, weight_out, out_left, out_right, stack):
    count = left.shape[0]
    stack[:count, :] = left[...]
    stack[count:, :] = right[...]
    part = products(stack[...], weight_in[0], weight_out[0], 0)
    out_left[...] = part[:count, :]
    out_right[...] = part[count:, :]


def gather_kernel(me, left, right, far, own, out):
    count = own.shape[0]
    groups = out.shape[0] // count
    for rows, step in ((left, 1), (right, 3), (far, 2), (own, 0)):
        group = lax.rem(me[0] + groups - step, groups)
        out[pl.ds(pl.multiple_of(group * count, count), count), :] = rows[...]


def residual_kernel(rows, pair, out):
    hidden = pair.shape[1] // 2
    out[...] = products(rows[...], pair[:, :hidden], pair[:, hidden:], 1)


def sum_kernel(own, left, right, far, out):
    total = own[...].astype(jnp.float32) + left[...].astype(jnp.float32)
    total = total + right[...].astype(jnp.float32) + far[...].astype(jnp.float32)
    out[...] = total.astype(jnp.bfloat16).reshape(out.shape)


def scale_kernel(res, tokens, weight, gate, out):
    model = res.shape[1]
    logit = jnp.sum(tokens[...].astype(jnp.float32) * weight[...].astype(jnp.float32), axis=1, keepdims=True)
    coef = 1.0 / (1.0 + jnp.exp(-logit))
    gates = jnp.transpose(jnp.broadcast_to(gate[...], (128, gate.shape[1])))
    out[:, :model] = coef * res[...].astype(jnp.float32)
    out[:, model:] = (1.0 - coef) * gates


def mix_kernel(routes, slots, scaled, out):
    experts, capacity, model = slots.shape
    table = slot_table(routes[...], capacity, experts * capacity)
    rows = slots[...].reshape(experts * capacity, model)
    expert_out = lax.dot_general(table, rows, (((0,), (0,)), ((), ())), preferred_element_type=jnp.float32)
    out[...] = (scaled[:, :model] + scaled[:, model : model + 1] * expert_out).astype(jnp.bfloat16)


def block(shape):
    return pl.BlockSpec(shape, lambda i: (0,) * len(shape))


def call(kernel, ins, shape, estimate=None, scratch=(), count=1, params=PARAMS, dtype=jnp.bfloat16):
    whole = jax.ShapeDtypeStruct(shape, dtype)
    return pl.pallas_call(
        kernel,
        grid=(1,),
        in_specs=[SMEM if value.ndim == 1 else block(value.shape) for value in ins],
        out_specs=block(shape) if count == 1 else [block(shape)] * count,
        out_shape=whole if count == 1 else [whole] * count,
        scratch_shapes=scratch,
        compiler_params=params,
        cost_estimate=estimate,
    )(*ins)


def shifted(value, step):
    size = lax.axis_size("grp")
    return lax.ppermute(value, "grp", [(i, (i + step) % size) for i in range(size)])


def across(value, axis):
    return lax.all_to_all(value, axis, split_axis=0, concat_axis=0, tiled=True)


def after(value, earlier):
    return lax.optimization_barrier((value, earlier))[0]


def local(tokens, routes, gate_prob, coef_weight, exp_up, exp_down, res_up, res_down):
    row_count, model = tokens.shape
    groups, experts = lax.axis_size("grp"), lax.axis_size("ep")
    capacity = 2 * row_count // experts
    slots = experts * capacity
    hidden = exp_up.shape[2]
    route_row = routes.reshape(1, row_count)

    res_pair = jnp.concatenate([res_up, res_down.T], axis=1)
    res_all = lax.all_gather(res_pair, "ep", axis=0, tiled=True)

    outgoing = call(dispatch_kernel, (route_row, tokens), (experts, capacity, model), params=WHOLE)
    arrived = across(outgoing, "ep")
    me = lax.axis_index("grp").astype(jnp.int32).reshape(1)
    other_tokens = [shifted(tokens, step) for step in (1, 3, 2)]
    whole_rows = call(gather_kernel, (me, *other_tokens, tokens), (groups * row_count, model))
    arrived = after(arrived, whole_rows)
    arrived = call(unpack_kernel, (arrived,), (slots, model))
    left, right, far = [shifted(arrived, step) for step in (1, 3, 2)]
    shape, weights = arrived.shape, (exp_up, exp_down)
    own = call(expert_kernel, (arrived, *weights), shape, cost(slots, model, hidden))
    left, right = call(
        expert_pair_kernel,
        (after(left, own), right, *weights),
        shape,
        cost(2 * slots, model, hidden),
        scratch=[pltpu.VMEM((2 * slots, model), jnp.bfloat16)],
        count=2,
    )
    part = call(expert_kernel, (after(far, left), *weights), shape, cost(slots, model, hidden))
    left, right, far = shifted(left, 3), shifted(right, 1), shifted(part, 2)

    total = call(sum_kernel, (own, left, right, far), (experts, capacity, model))
    res_part = call(
        residual_kernel,
        (after(whole_rows, total), res_all),
        whole_rows.shape,
        cost(groups * row_count, model, hidden),
    )
    res_out = lax.psum_scatter(res_part, "grp", scatter_dimension=0, tiled=True)
    total = after(total, res_part)
    returned = across(total, "ep")
    scaled = call(
        scale_kernel,
        (res_out, tokens, coef_weight.reshape(1, model), gate_prob.reshape(1, row_count)),
        (row_count, model + 128),
        dtype=jnp.float32,
    )
    return call(mix_kernel, (route_row, after(returned, scaled), scaled), (row_count, model))


def solution(mesh):
    in_specs = (
        P(("grp", "ep"), None),
        P(("grp", "ep"), None),
        P(("grp", "ep")),
        P(),
        P("ep", None, "grp"),
        P("ep", "grp", None),
        P("ep", "grp"),
        P("grp", "ep"),
    )
    out_specs = P(("grp", "ep"), None)
    return jax.shard_map(local, mesh=mesh, in_specs=in_specs, out_specs=out_specs, check_vma=False)
```

```python
import functools

import jax
import jax.numpy as jnp
from jax import lax
from jax.experimental import pallas as pl
from jax.experimental.pallas import tpu as pltpu
from jax.sharding import PartitionSpec as P

SMEM = pl.BlockSpec(memory_space=pltpu.SMEM)
PARAMS = pltpu.CompilerParams(vmem_limit_bytes=48 * 1024 * 1024)
WHOLE = pltpu.CompilerParams(vmem_limit_bytes=60 * 1024 * 1024)


def cost(rows, model, hidden):
    return pl.CostEstimate(
        flops=4 * rows * model * hidden,
        bytes_accessed=4 * model * (hidden + rows),
        transcendentals=rows * hidden,
    )


def slot_table(route_row, capacity, slots):
    count = route_row.shape[1]
    route = jnp.broadcast_to(route_row, (count, count))
    earlier = lax.broadcasted_iota(jnp.int32, (count, count), 0) < lax.broadcasted_iota(jnp.int32, (count, count), 1)
    place = jnp.sum(jnp.where((route == jnp.transpose(route)) & earlier, 1, 0), axis=0, keepdims=True)
    slot = jnp.broadcast_to(route_row * capacity + place, (slots, count))
    return jnp.where(lax.broadcasted_iota(jnp.int32, (slots, count), 0) == slot, 1.0, 0.0).astype(jnp.bfloat16)


def dispatch_kernel(routes, tokens, out):
    experts, capacity, model = out.shape
    table = slot_table(routes[...], capacity, experts * capacity)
    rows = jnp.dot(table, tokens[...], preferred_element_type=jnp.float32).astype(jnp.bfloat16)
    out[...] = rows.reshape(experts, capacity, model)


def unpack_kernel(slots, out):
    out[...] = slots[...].reshape(out.shape)


def products(rows, weight_in, weight_out, out_dim):
    product = jnp.dot(rows, weight_in, preferred_element_type=jnp.float32)
    hidden = jax.nn.gelu(product, approximate=True).astype(jnp.bfloat16)
    part = lax.dot_general(
        hidden, weight_out, (((1,), (out_dim,)), ((), ())), preferred_element_type=jnp.float32
    )
    return part.astype(jnp.bfloat16)


def expert_kernel(rows, weight_in, weight_out, out):
    out[...] = products(rows[...], weight_in[0], weight_out[0], 0)


def expert_halves_kernel(upper, lower, weight_in, weight_out, out, stack):
    count = upper.shape[0]
    stack[:count, :] = upper[...]
    stack[count:, :] = lower[...]
    out[...] = products(stack[...], weight_in[0], weight_out[0], 0)


def expert_pair_kernel(left, right, weight_in, weight_out, out_left, out_right, stack):
    count = left.shape[0]
    stack[:count, :] = left[...]
    stack[count:, :] = right[...]
    part = products(stack[...], weight_in[0], weight_out[0], 0)
    out_left[...] = part[:count, :]
    out_right[...] = part[count:, :]


def gather_kernel(left, right, far, own, out):
    count = own.shape[0]
    for place, rows in enumerate((left, right, far, own)):
        out[place * count : (place + 1) * count, :] = rows[...]


def residual_kernel(rows, pair, *outs):
    hidden = pair.shape[1] // 2
    part = products(rows[...], pair[:, :hidden], pair[:, hidden:], 1)
    count = part.shape[0] // len(outs)
    for place, out in enumerate(outs):
        out[...] = part[place * count : (place + 1) * count, :]


def sum_kernel(own, left, right, far, out):
    total = own[...].astype(jnp.float32) + left[...].astype(jnp.float32)
    total = total + right[...].astype(jnp.float32) + far[...].astype(jnp.float32)
    out[...] = total.astype(jnp.bfloat16).reshape(out.shape)


def scale_kernel(left, right, far, own, tokens, weight, gate, out):
    model = own.shape[1]
    res = left[...].astype(jnp.float32) + right[...].astype(jnp.float32)
    res = res + far[...].astype(jnp.float32) + own[...].astype(jnp.float32)
    logit = jnp.sum(tokens[...].astype(jnp.float32) * weight[...].astype(jnp.float32), axis=1, keepdims=True)
    coef = 1.0 / (1.0 + jnp.exp(-logit))
    gates = jnp.transpose(jnp.broadcast_to(gate[...], (128, gate.shape[1])))
    out[:, :model] = coef * res
    out[:, model:] = (1.0 - coef) * gates


def mix_kernel(routes, slots, scaled, out):
    experts, capacity, model = slots.shape
    table = slot_table(routes[...], capacity, experts * capacity)
    rows = slots[...].reshape(experts * capacity, model)
    expert_out = lax.dot_general(table, rows, (((0,), (0,)), ((), ())), preferred_element_type=jnp.float32)
    out[...] = (scaled[:, :model] + scaled[:, model : model + 1] * expert_out).astype(jnp.bfloat16)


def block(shape):
    return pl.BlockSpec(shape, lambda i: (0,) * len(shape))


def call(kernel, ins, shape, estimate=None, scratch=(), count=1, params=PARAMS, dtype=jnp.bfloat16):
    whole = jax.ShapeDtypeStruct(shape, dtype)
    return pl.pallas_call(
        kernel,
        grid=(1,),
        in_specs=[SMEM if value.ndim == 1 else block(value.shape) for value in ins],
        out_specs=block(shape) if count == 1 else [block(shape)] * count,
        out_shape=whole if count == 1 else [whole] * count,
        scratch_shapes=scratch,
        compiler_params=params,
        cost_estimate=estimate,
    )(*ins)


def shifted(value, step):
    size = lax.axis_size("grp")
    return lax.ppermute(value, "grp", [(i, (i + step) % size) for i in range(size)])


def across(value, axis):
    return lax.all_to_all(value, axis, split_axis=0, concat_axis=0, tiled=True)


def after(value, earlier):
    return lax.optimization_barrier((value, earlier))[0]


def local(tokens, routes, gate_prob, coef_weight, exp_up, exp_down, res_up, res_down):
    row_count, model = tokens.shape
    groups, experts = lax.axis_size("grp"), lax.axis_size("ep")
    capacity = 2 * row_count // experts
    slots = experts * capacity
    hidden = exp_up.shape[2]
    route_row = routes.reshape(1, row_count)

    res_pair = jnp.concatenate([res_up, res_down.T], axis=1)
    res_all = lax.all_gather(res_pair, "ep", axis=0, tiled=True)

    outgoing = call(dispatch_kernel, (route_row, tokens), (experts, capacity, model), params=WHOLE)
    arrived = across(outgoing, "ep")
    other_tokens = [shifted(tokens, step) for step in (1, 3, 2)]
    arrived = after(arrived, other_tokens)
    arrived = call(unpack_kernel, (arrived,), (slots, model))
    left, right = shifted(arrived, 1), shifted(arrived, 3)
    half, shape, weights = slots // 2, arrived.shape, (exp_up, exp_down)
    whole_rows = call(gather_kernel, (*other_tokens, tokens), (groups * row_count, model))
    own = call(expert_kernel, (after(arrived, whole_rows), *weights), shape, cost(slots, model, hidden))
    left, right = after((left, right), own)
    upper, lower = shifted(left[:half], 1), shifted(right[half:], 3)
    near_left, near_right = call(
        expert_pair_kernel,
        (left, right, *weights),
        shape,
        cost(2 * slots, model, hidden),
        scratch=[pltpu.VMEM((2 * slots, model), jnp.bfloat16)],
        count=2,
    )
    far = call(
        expert_halves_kernel,
        (after(upper, near_left), lower, *weights),
        shape,
        cost(slots, model, hidden),
        scratch=[pltpu.VMEM(shape, jnp.bfloat16)],
    )
    left, right, far_back = shifted(near_left, 3), shifted(near_right, 1), shifted(far, 2)

    res_parts = call(
        residual_kernel,
        (after(whole_rows, far), res_all),
        (row_count, model),
        cost(groups * row_count, model, hidden),
        count=groups,
        params=WHOLE,
    )
    total = call(sum_kernel, (own, left, after(right, res_parts), far_back), (experts, capacity, model))
    res_parts = after(res_parts, total)
    res_parts = [shifted(part, step) for part, step in zip(res_parts, (3, 1, 2))] + [res_parts[3]]
    returned = across(total, "ep")
    scaled = call(
        scale_kernel,
        (*res_parts, tokens, coef_weight.reshape(1, model), gate_prob.reshape(1, row_count)),
        (row_count, model + 128),
        dtype=jnp.float32,
    )
    return call(mix_kernel, (route_row, after(returned, scaled), scaled), (row_count, model))


def solution(mesh):
    in_specs = (
        P(("grp", "ep"), None),
        P(("grp", "ep"), None),
        P(("grp", "ep")),
        P(),
        P("ep", None, "grp"),
        P("ep", "grp", None),
        P("ep", "grp"),
        P("grp", "ep"),
    )
    out_specs = P(("grp", "ep"), None)
    return jax.shard_map(local, mesh=mesh, in_specs=in_specs, out_specs=out_specs, check_vma=False)
```

```python
import functools

import jax
import jax.numpy as jnp
from jax import lax
from jax.experimental import pallas as pl
from jax.experimental.pallas import tpu as pltpu
from jax.sharding import PartitionSpec as P

SMEM = pl.BlockSpec(memory_space=pltpu.SMEM)
PARAMS = pltpu.CompilerParams(vmem_limit_bytes=48 * 1024 * 1024)
WHOLE = pltpu.CompilerParams(vmem_limit_bytes=60 * 1024 * 1024)


def cost(rows, model, hidden):
    return pl.CostEstimate(
        flops=4 * rows * model * hidden,
        bytes_accessed=4 * model * (hidden + rows),
        transcendentals=rows * hidden,
    )


def slot_table(route_row, capacity, slots):
    count = route_row.shape[1]
    route = jnp.broadcast_to(route_row, (count, count))
    earlier = lax.broadcasted_iota(jnp.int32, (count, count), 0) < lax.broadcasted_iota(jnp.int32, (count, count), 1)
    place = jnp.sum(jnp.where((route == jnp.transpose(route)) & earlier, 1, 0), axis=0, keepdims=True)
    slot = jnp.broadcast_to(route_row * capacity + place, (slots, count))
    return jnp.where(lax.broadcasted_iota(jnp.int32, (slots, count), 0) == slot, 1.0, 0.0).astype(jnp.bfloat16)


def dispatch_kernel(routes, tokens, out):
    experts, capacity, model = out.shape
    table = slot_table(routes[...], capacity, experts * capacity)
    rows = jnp.dot(table, tokens[...], preferred_element_type=jnp.float32).astype(jnp.bfloat16)
    out[...] = rows.reshape(experts, capacity, model)


def unpack_kernel(slots, out):
    out[...] = slots[...].reshape(out.shape)


def products(rows, weight_in, weight_out, out_dim):
    product = jnp.dot(rows, weight_in, preferred_element_type=jnp.float32)
    hidden = jax.nn.gelu(product, approximate=True).astype(jnp.bfloat16)
    part = lax.dot_general(
        hidden, weight_out, (((1,), (out_dim,)), ((), ())), preferred_element_type=jnp.float32
    )
    return part.astype(jnp.bfloat16)


def expert_kernel(rows, weight_in, weight_out, out):
    out[...] = products(rows[...], weight_in[0], weight_out[0], 0)


def expert_halves_kernel(upper, lower, weight_in, weight_out, out, stack):
    count = upper.shape[0]
    stack[:count, :] = upper[...]
    stack[count:, :] = lower[...]
    out[...] = products(stack[...], weight_in[0], weight_out[0], 0)


def expert_pair_kernel(left, right, weight_in, weight_out, out_left, out_right, stack):
    count = left.shape[0]
    stack[:count, :] = left[...]
    stack[count:, :] = right[...]
    part = products(stack[...], weight_in[0], weight_out[0], 0)
    out_left[...] = part[:count, :]
    out_right[...] = part[count:, :]


def gather_kernel(left, right, far, own, out):
    count = own.shape[0]
    for place, rows in enumerate((left, right, far, own)):
        out[place * count : (place + 1) * count, :] = rows[...]


def residual_kernel(me, rows, pair, out):
    hidden = pair.shape[1] // 2
    part = products(rows[...], pair[:, :hidden], pair[:, hidden:], 1)
    steps = (1, 3, 2, 0)
    count = part.shape[0] // len(steps)
    for place, step in enumerate(steps):
        group = lax.rem(me[0] + len(steps) - step, len(steps))
        out[pl.ds(pl.multiple_of(group * count, count), count), :] = part[place * count : (place + 1) * count, :]


def sum_kernel(own, left, right, far, out):
    total = own[...].astype(jnp.float32) + left[...].astype(jnp.float32)
    total = total + right[...].astype(jnp.float32) + far[...].astype(jnp.float32)
    out[...] = total.astype(jnp.bfloat16).reshape(out.shape)


def scale_kernel(res, tokens, weight, gate, out):
    model = res.shape[1]
    logit = jnp.sum(tokens[...].astype(jnp.float32) * weight[...].astype(jnp.float32), axis=1, keepdims=True)
    coef = 1.0 / (1.0 + jnp.exp(-logit))
    gates = jnp.transpose(jnp.broadcast_to(gate[...], (128, gate.shape[1])))
    out[:, :model] = coef * res[...].astype(jnp.float32)
    out[:, model:] = (1.0 - coef) * gates


def mix_kernel(routes, slots, scaled, out):
    experts, capacity, model = slots.shape
    table = slot_table(routes[...], capacity, experts * capacity)
    rows = slots[...].reshape(experts * capacity, model)
    expert_out = lax.dot_general(table, rows, (((0,), (0,)), ((), ())), preferred_element_type=jnp.float32)
    out[...] = (scaled[:, :model] + scaled[:, model : model + 1] * expert_out).astype(jnp.bfloat16)


def block(shape):
    return pl.BlockSpec(shape, lambda i: (0,) * len(shape))


def call(kernel, ins, shape, estimate=None, scratch=(), count=1, params=PARAMS, dtype=jnp.bfloat16):
    whole = jax.ShapeDtypeStruct(shape, dtype)
    return pl.pallas_call(
        kernel,
        grid=(1,),
        in_specs=[SMEM if value.ndim == 1 else block(value.shape) for value in ins],
        out_specs=block(shape) if count == 1 else [block(shape)] * count,
        out_shape=whole if count == 1 else [whole] * count,
        scratch_shapes=scratch,
        compiler_params=params,
        cost_estimate=estimate,
    )(*ins)


def shifted(value, step):
    size = lax.axis_size("grp")
    return lax.ppermute(value, "grp", [(i, (i + step) % size) for i in range(size)])


def across(value, axis):
    return lax.all_to_all(value, axis, split_axis=0, concat_axis=0, tiled=True)


def after(value, earlier):
    return lax.optimization_barrier((value, earlier))[0]


def local(tokens, routes, gate_prob, coef_weight, exp_up, exp_down, res_up, res_down):
    row_count, model = tokens.shape
    groups, experts = lax.axis_size("grp"), lax.axis_size("ep")
    capacity = 2 * row_count // experts
    slots = experts * capacity
    hidden = exp_up.shape[2]
    route_row = routes.reshape(1, row_count)

    res_pair = jnp.concatenate([res_up, res_down.T], axis=1)
    res_all = lax.all_gather(res_pair, "ep", axis=0, tiled=True)

    outgoing = call(dispatch_kernel, (route_row, tokens), (experts, capacity, model), params=WHOLE)
    arrived = across(outgoing, "ep")
    other_tokens = [shifted(tokens, step) for step in (1, 3, 2)]
    arrived = after(arrived, other_tokens)
    arrived = call(unpack_kernel, (arrived,), (slots, model))
    left, right = shifted(arrived, 1), shifted(arrived, 3)
    half, shape, weights = slots // 2, arrived.shape, (exp_up, exp_down)
    whole_rows = call(gather_kernel, (*other_tokens, tokens), (groups * row_count, model))
    own = call(expert_kernel, (after(arrived, whole_rows), *weights), shape, cost(slots, model, hidden))
    left, right = after((left, right), own)
    upper, lower = shifted(left[:half], 1), shifted(right[half:], 3)
    near_left, near_right = call(
        expert_pair_kernel,
        (left, right, *weights),
        shape,
        cost(2 * slots, model, hidden),
        scratch=[pltpu.VMEM((2 * slots, model), jnp.bfloat16)],
        count=2,
    )
    far = call(
        expert_halves_kernel,
        (after(upper, near_left), lower, *weights),
        shape,
        cost(slots, model, hidden),
        scratch=[pltpu.VMEM(shape, jnp.bfloat16)],
    )
    left, right, far_back = shifted(near_left, 3), shifted(near_right, 1), shifted(far, 2)

    me = lax.axis_index("grp").astype(jnp.int32).reshape(1)
    res_part = call(
        residual_kernel,
        (me, after(whole_rows, far), res_all),
        whole_rows.shape,
        cost(groups * row_count, model, hidden),
        params=WHOLE,
    )
    res_out = lax.psum_scatter(res_part, "grp", scatter_dimension=0, tiled=True)
    total = call(
        sum_kernel,
        (own, left, after(right, res_part), far_back),
        (experts, capacity, model),
        cost(64 * slots, model, hidden),
    )
    returned = across(total, "ep")
    scaled = call(
        scale_kernel,
        (res_out, tokens, coef_weight.reshape(1, model), gate_prob.reshape(1, row_count)),
        (row_count, model + 128),
        dtype=jnp.float32,
    )
    return call(mix_kernel, (route_row, after(returned, scaled), scaled), (row_count, model))


def solution(mesh):
    in_specs = (
        P(("grp", "ep"), None),
        P(("grp", "ep"), None),
        P(("grp", "ep")),
        P(),
        P("ep", None, "grp"),
        P("ep", "grp", None),
        P("ep", "grp"),
        P("grp", "ep"),
    )
    out_specs = P(("grp", "ep"), None)
    return jax.shard_map(local, mesh=mesh, in_specs=in_specs, out_specs=out_specs, check_vma=False)
```

```python
import functools

import jax
import jax.numpy as jnp
from jax import lax
from jax.experimental import pallas as pl
from jax.experimental.pallas import tpu as pltpu
from jax.sharding import PartitionSpec as P

SMEM = pl.BlockSpec(memory_space=pltpu.SMEM)
PARAMS = pltpu.CompilerParams(vmem_limit_bytes=48 * 1024 * 1024)
WHOLE = pltpu.CompilerParams(vmem_limit_bytes=60 * 1024 * 1024)


def cost(rows, model, hidden):
    return pl.CostEstimate(
        flops=4 * rows * model * hidden,
        bytes_accessed=4 * model * (hidden + rows),
        transcendentals=rows * hidden,
    )


def slot_table(route_row, capacity, slots):
    count = route_row.shape[1]
    route = jnp.broadcast_to(route_row, (count, count))
    earlier = lax.broadcasted_iota(jnp.int32, (count, count), 0) < lax.broadcasted_iota(jnp.int32, (count, count), 1)
    place = jnp.sum(jnp.where((route == jnp.transpose(route)) & earlier, 1, 0), axis=0, keepdims=True)
    slot = jnp.broadcast_to(route_row * capacity + place, (slots, count))
    return jnp.where(lax.broadcasted_iota(jnp.int32, (slots, count), 0) == slot, 1.0, 0.0).astype(jnp.bfloat16)


def dispatch_kernel(routes, tokens, out):
    experts, capacity, model = out.shape
    table = slot_table(routes[...], capacity, experts * capacity)
    rows = jnp.dot(table, tokens[...], preferred_element_type=jnp.float32).astype(jnp.bfloat16)
    out[...] = rows.reshape(experts, capacity, model)


def unpack_kernel(slots, out):
    out[...] = slots[...].reshape(out.shape)


def products(rows, weight_in, weight_out, out_dim):
    product = jnp.dot(rows, weight_in, preferred_element_type=jnp.float32)
    hidden = jax.nn.gelu(product, approximate=True).astype(jnp.bfloat16)
    part = lax.dot_general(
        hidden, weight_out, (((1,), (out_dim,)), ((), ())), preferred_element_type=jnp.float32
    )
    return part.astype(jnp.bfloat16)


def expert_kernel(rows, weight_in, weight_out, out):
    out[...] = products(rows[...], weight_in[0], weight_out[0], 0)


def expert_halves_kernel(upper, lower, weight_in, weight_out, out, stack):
    count = upper.shape[0]
    stack[:count, :] = upper[...]
    stack[count:, :] = lower[...]
    out[...] = products(stack[...], weight_in[0], weight_out[0], 0)


def expert_pair_kernel(left, right, weight_in, weight_out, out_left, out_right, stack):
    count = left.shape[0]
    stack[:count, :] = left[...]
    stack[count:, :] = right[...]
    part = products(stack[...], weight_in[0], weight_out[0], 0)
    out_left[...] = part[:count, :]
    out_right[...] = part[count:, :]


def gather_kernel(left, right, far, own, out):
    count = own.shape[0]
    for place, rows in enumerate((left, right, far, own)):
        out[place * count : (place + 1) * count, :] = rows[...]


def residual_kernel(me, rows, pair, out, held, weight_in, weight_out, made, sems):
    steps = (1, 3, 2, 0)
    cuts, model = 4, weight_in.shape[0]
    count, width, hidden = held.shape[0] // len(steps), model // cuts, weight_in.shape[1]
    blocks = [slice(k * width, (k + 1) * width) for k in range(cuts)]
    rows_in = pltpu.make_async_copy(rows, held, sems.at[0])
    first = [
        pltpu.make_async_copy(pair.at[cut, :hidden], weight_in.at[cut, :], sems.at[1 + k])
        for k, cut in enumerate(blocks)
    ]
    second = pltpu.make_async_copy(pair.at[:, hidden:], weight_out, sems.at[1 + cuts])
    for copy in (rows_in, *first, second):
        copy.start()
    rows_in.wait()
    product = None
    for cut, copy in zip(blocks, first):
        copy.wait()
        term = jnp.dot(held[:, cut], weight_in[cut, :], preferred_element_type=jnp.float32)
        product = term if product is None else product + term
    units = jax.nn.gelu(product, approximate=True).astype(jnp.bfloat16)
    second.wait()
    sent = []
    for side in range(2):
        part = lax.dot_general(
            units[side * 2 * count : (side + 1) * 2 * count, :],
            weight_out[...],
            (((1,), (1,)), ((), ())),
            preferred_element_type=jnp.float32,
        ).astype(jnp.bfloat16)
        for place in (2 * side, 2 * side + 1):
            own = slice(place * count, (place + 1) * count)
            made[own, :] = part[(place - 2 * side) * count : (place - 2 * side + 1) * count, :]
            group = lax.rem(me[0] + len(steps) - steps[place], len(steps))
            target = out.at[pl.ds(pl.multiple_of(group * count, count), count), :]
            copy = pltpu.make_async_copy(made.at[own, :], target, sems.at[2 + cuts + place])
            copy.start()
            sent.append(copy)
    for copy in sent:
        copy.wait()


def sum_kernel(own, left, right, far, out):
    total = own[...].astype(jnp.float32) + left[...].astype(jnp.float32)
    total = total + right[...].astype(jnp.float32) + far[...].astype(jnp.float32)
    out[...] = total.astype(jnp.bfloat16).reshape(out.shape)


def scale_kernel(res, tokens, weight, gate, out):
    model = res.shape[1]
    logit = jnp.sum(tokens[...].astype(jnp.float32) * weight[...].astype(jnp.float32), axis=1, keepdims=True)
    coef = 1.0 / (1.0 + jnp.exp(-logit))
    gates = jnp.transpose(jnp.broadcast_to(gate[...], (128, gate.shape[1])))
    out[:, :model] = coef * res[...].astype(jnp.float32)
    out[:, model:] = (1.0 - coef) * gates


def mix_kernel(routes, slots, scaled, out):
    experts, capacity, model = slots.shape
    table = slot_table(routes[...], capacity, experts * capacity)
    rows = slots[...].reshape(experts * capacity, model)
    expert_out = lax.dot_general(table, rows, (((0,), (0,)), ((), ())), preferred_element_type=jnp.float32)
    out[...] = (scaled[:, :model] + scaled[:, model : model + 1] * expert_out).astype(jnp.bfloat16)


def block(shape):
    return pl.BlockSpec(shape, lambda i: (0,) * len(shape))


def call(kernel, ins, shape, estimate=None, scratch=(), count=1, params=PARAMS, dtype=jnp.bfloat16):
    whole = jax.ShapeDtypeStruct(shape, dtype)
    return pl.pallas_call(
        kernel,
        grid=(1,),
        in_specs=[SMEM if value.ndim == 1 else block(value.shape) for value in ins],
        out_specs=block(shape) if count == 1 else [block(shape)] * count,
        out_shape=whole if count == 1 else [whole] * count,
        scratch_shapes=scratch,
        compiler_params=params,
        cost_estimate=estimate,
    )(*ins)


def shifted(value, step):
    size = lax.axis_size("grp")
    return lax.ppermute(value, "grp", [(i, (i + step) % size) for i in range(size)])


def across(value, axis):
    return lax.all_to_all(value, axis, split_axis=0, concat_axis=0, tiled=True)


def after(value, earlier):
    return lax.optimization_barrier((value, earlier))[0]


def local(tokens, routes, gate_prob, coef_weight, exp_up, exp_down, res_up, res_down):
    row_count, model = tokens.shape
    groups, experts = lax.axis_size("grp"), lax.axis_size("ep")
    capacity = 2 * row_count // experts
    slots = experts * capacity
    hidden = exp_up.shape[2]
    route_row = routes.reshape(1, row_count)

    res_pair = jnp.concatenate([res_up, res_down.T], axis=1)
    res_all = lax.all_gather(res_pair, "ep", axis=0, tiled=True)

    outgoing = call(dispatch_kernel, (route_row, tokens), (experts, capacity, model), params=WHOLE)
    arrived = across(outgoing, "ep")
    other_tokens = [shifted(tokens, step) for step in (1, 3, 2)]
    arrived = after(arrived, other_tokens)
    arrived = call(unpack_kernel, (arrived,), (slots, model))
    left, right = shifted(arrived, 1), shifted(arrived, 3)
    half, shape, weights = slots // 2, arrived.shape, (exp_up, exp_down)
    whole_rows = call(gather_kernel, (*other_tokens, tokens), (groups * row_count, model))
    own = call(expert_kernel, (after(arrived, whole_rows), *weights), shape, cost(slots, model, hidden))
    left, right = after((left, right), own)
    upper, lower = shifted(left[:half], 1), shifted(right[half:], 3)
    near_left, near_right = call(
        expert_pair_kernel,
        (left, right, *weights),
        shape,
        cost(2 * slots, model, hidden),
        scratch=[pltpu.VMEM((2 * slots, model), jnp.bfloat16)],
        count=2,
    )
    far = call(
        expert_halves_kernel,
        (after(upper, near_left), lower, *weights),
        shape,
        cost(slots, model, hidden),
        scratch=[pltpu.VMEM(shape, jnp.bfloat16)],
    )
    left, right, far_back = shifted(near_left, 3), shifted(near_right, 1), shifted(far, 2)

    me = lax.axis_index("grp").astype(jnp.int32).reshape(1)
    anywhere = pl.BlockSpec(memory_space=pl.ANY)
    res_part = pl.pallas_call(
        residual_kernel,
        in_specs=[SMEM, anywhere, anywhere],
        out_specs=anywhere,
        out_shape=jax.ShapeDtypeStruct(whole_rows.shape, jnp.bfloat16),
        scratch_shapes=[
            pltpu.VMEM(whole_rows.shape, jnp.bfloat16),
            pltpu.VMEM((model, hidden), jnp.bfloat16),
            pltpu.VMEM((model, hidden), jnp.bfloat16),
            pltpu.VMEM(whole_rows.shape, jnp.bfloat16),
            pltpu.SemaphoreType.DMA((10,)),
        ],
        compiler_params=WHOLE,
        cost_estimate=cost(groups * row_count, model, hidden),
    )(me, after(whole_rows, far), res_all)
    res_out = lax.psum_scatter(res_part, "grp", scatter_dimension=0, tiled=True)
    row_block = pl.BlockSpec((slots // 2, model), lambda i: (i, 0))
    total = pl.pallas_call(
        sum_kernel,
        grid=(2,),
        in_specs=[row_block] * 4,
        out_specs=pl.BlockSpec((experts // 2, capacity, model), lambda i: (i, 0, 0)),
        out_shape=jax.ShapeDtypeStruct((experts, capacity, model), jnp.bfloat16),
        compiler_params=PARAMS,
        cost_estimate=cost(64 * slots, model, hidden),
    )(own, left, after(right, res_part), far_back)
    returned = across(total, "ep")
    scaled = call(
        scale_kernel,
        (res_out, tokens, coef_weight.reshape(1, model), gate_prob.reshape(1, row_count)),
        (row_count, model + 128),
        dtype=jnp.float32,
    )
    return call(mix_kernel, (route_row, after(returned, scaled), scaled), (row_count, model))


def solution(mesh):
    in_specs = (
        P(("grp", "ep"), None),
        P(("grp", "ep"), None),
        P(("grp", "ep")),
        P(),
        P("ep", None, "grp"),
        P("ep", "grp", None),
        P("ep", "grp"),
        P("grp", "ep"),
    )
    out_specs = P(("grp", "ep"), None)
    return jax.shard_map(local, mesh=mesh, in_specs=in_specs, out_specs=out_specs, check_vma=False)
```

```python
import functools

import jax
import jax.numpy as jnp
from jax import lax
from jax.experimental import pallas as pl
from jax.experimental.pallas import tpu as pltpu
from jax.sharding import PartitionSpec as P

SMEM = pl.BlockSpec(memory_space=pltpu.SMEM)
PARAMS = pltpu.CompilerParams(vmem_limit_bytes=48 * 1024 * 1024)
WHOLE = pltpu.CompilerParams(vmem_limit_bytes=60 * 1024 * 1024)


def cost(rows, model, hidden):
    return pl.CostEstimate(
        flops=4 * rows * model * hidden,
        bytes_accessed=4 * model * (hidden + rows),
        transcendentals=rows * hidden,
    )


def slot_table(route_row, capacity, slots):
    count = route_row.shape[1]
    route = jnp.broadcast_to(route_row, (count, count))
    earlier = lax.broadcasted_iota(jnp.int32, (count, count), 0) < lax.broadcasted_iota(jnp.int32, (count, count), 1)
    place = jnp.sum(jnp.where((route == jnp.transpose(route)) & earlier, 1, 0), axis=0, keepdims=True)
    slot = jnp.broadcast_to(route_row * capacity + place, (slots, count))
    return jnp.where(lax.broadcasted_iota(jnp.int32, (slots, count), 0) == slot, 1.0, 0.0).astype(jnp.bfloat16)


def dispatch_kernel(routes, tokens, out):
    experts, capacity, model = out.shape
    table = slot_table(routes[...], capacity, experts * capacity)
    rows = jnp.dot(table, tokens[...], preferred_element_type=jnp.float32).astype(jnp.bfloat16)
    out[...] = rows.reshape(experts, capacity, model)


def join_kernel(left, right, out):
    width = left.shape[1]
    out[:, :width] = left[...]
    out[:, width:] = right[...]


def unpack_kernel(slots, out):
    out[...] = slots[...].reshape(out.shape)


def products(rows, weight_in, weight_out, out_dim):
    product = jnp.dot(rows, weight_in, preferred_element_type=jnp.float32)
    hidden = jax.nn.gelu(product, approximate=True).astype(jnp.bfloat16)
    part = lax.dot_general(
        hidden, weight_out, (((1,), (out_dim,)), ((), ())), preferred_element_type=jnp.float32
    )
    return part.astype(jnp.bfloat16)


def expert_kernel(rows, weight_in, weight_out, out):
    out[...] = products(rows[...], weight_in[0], weight_out[0], 0)


def expert_halves_kernel(upper, lower, weight_in, weight_out, out, stack):
    count = upper.shape[0]
    stack[:count, :] = upper[...]
    stack[count:, :] = lower[...]
    out[...] = products(stack[...], weight_in[0], weight_out[0], 0)


def expert_pair_kernel(left, right, weight_in, weight_out, out_left, out_right, stack):
    count = left.shape[0]
    stack[:count, :] = left[...]
    stack[count:, :] = right[...]
    part = products(stack[...], weight_in[0], weight_out[0], 0)
    out_left[...] = part[:count, :]
    out_right[...] = part[count:, :]


def gather_kernel(left, right, far, own, out):
    count = own.shape[0]
    for place, rows in enumerate((left, right, far, own)):
        out[place * count : (place + 1) * count, :] = rows[...]


def residual_kernel(rows, pair, *outs):
    hidden = pair.shape[1] // 2
    part = products(rows[...], pair[:, :hidden], pair[:, hidden:], 1)
    count = part.shape[0] // len(outs)
    for place, out in enumerate(outs):
        out[...] = part[place * count : (place + 1) * count, :]


def sum_kernel(own, left, right, far, out):
    total = own[...].astype(jnp.float32) + left[...].astype(jnp.float32)
    total = total + right[...].astype(jnp.float32) + far[...].astype(jnp.float32)
    out[...] = total.astype(jnp.bfloat16).reshape(out.shape)


def scale_kernel(far, left, right, own, tokens, weight, gate, out):
    model = own.shape[1]
    res = left[...].astype(jnp.float32) + right[...].astype(jnp.float32)
    res = res + far[...].astype(jnp.float32) + own[...].astype(jnp.float32)
    logit = jnp.sum(tokens[...].astype(jnp.float32) * weight[...].astype(jnp.float32), axis=1, keepdims=True)
    coef = 1.0 / (1.0 + jnp.exp(-logit))
    gates = jnp.transpose(jnp.broadcast_to(gate[...], (128, gate.shape[1])))
    out[:, :model] = coef * res
    out[:, model:] = (1.0 - coef) * gates


def mix_kernel(routes, slots, scaled, out):
    experts, capacity, model = slots.shape
    table = slot_table(routes[...], capacity, experts * capacity)
    rows = slots[...].reshape(experts * capacity, model)
    expert_out = lax.dot_general(table, rows, (((0,), (0,)), ((), ())), preferred_element_type=jnp.float32)
    out[...] = (scaled[:, :model] + scaled[:, model : model + 1] * expert_out).astype(jnp.bfloat16)


def block(shape):
    return pl.BlockSpec(shape, lambda i: (0,) * len(shape))


def call(kernel, ins, shape, estimate=None, scratch=(), count=1, params=PARAMS, dtype=jnp.bfloat16):
    whole = jax.ShapeDtypeStruct(shape, dtype)
    return pl.pallas_call(
        kernel,
        grid=(1,),
        in_specs=[SMEM if value.ndim == 1 else block(value.shape) for value in ins],
        out_specs=block(shape) if count == 1 else [block(shape)] * count,
        out_shape=whole if count == 1 else [whole] * count,
        scratch_shapes=scratch,
        compiler_params=params,
        cost_estimate=estimate,
    )(*ins)


def shifted(value, step):
    size = lax.axis_size("grp")
    return lax.ppermute(value, "grp", [(i, (i + step) % size) for i in range(size)])


def across(value, axis):
    return lax.all_to_all(value, axis, split_axis=0, concat_axis=0, tiled=True)


def after(value, earlier):
    return lax.optimization_barrier((value, earlier))[0]


def local(tokens, routes, gate_prob, coef_weight, exp_up, exp_down, res_up, res_down):
    row_count, model = tokens.shape
    groups, experts = lax.axis_size("grp"), lax.axis_size("ep")
    capacity = 2 * row_count // experts
    slots = experts * capacity
    hidden = exp_up.shape[2]
    route_row = routes.reshape(1, row_count)

    res_pair = call(join_kernel, (res_up, res_down.T), (res_up.shape[0], 2 * hidden), params=WHOLE)
    res_all = lax.all_gather(res_pair, "ep", axis=0, tiled=True)

    outgoing = call(dispatch_kernel, (route_row, tokens), (experts, capacity, model), params=WHOLE)
    arrived = across(outgoing, "ep")
    other_tokens = [shifted(tokens, step) for step in (1, 3, 2)]
    arrived = after(arrived, other_tokens)
    arrived = call(unpack_kernel, (arrived,), (slots, model))
    left, right = shifted(arrived, 1), shifted(arrived, 3)
    half, shape, weights = slots // 2, arrived.shape, (exp_up, exp_down)
    whole_rows = call(gather_kernel, (*other_tokens, tokens), (groups * row_count, model))
    own = call(expert_kernel, (after(arrived, whole_rows), *weights), shape, cost(slots, model, hidden))
    left, right = after((left, right), own)
    upper, lower = shifted(left[:half], 1), shifted(right[half:], 3)
    near_left, near_right = call(
        expert_pair_kernel,
        (left, right, *weights),
        shape,
        cost(2 * slots, model, hidden),
        scratch=[pltpu.VMEM((2 * slots, model), jnp.bfloat16)],
        count=2,
    )
    far = call(
        expert_halves_kernel,
        (after(upper, near_left), lower, *weights),
        shape,
        cost(slots, model, hidden),
        scratch=[pltpu.VMEM(shape, jnp.bfloat16)],
    )
    left, right, far_back = shifted(near_left, 3), shifted(near_right, 1), shifted(far, 2)

    res_parts = call(
        residual_kernel,
        (after(whole_rows, far), res_all),
        (row_count, model),
        cost(groups * row_count, model, hidden),
        count=groups,
        params=WHOLE,
    )
    total = call(sum_kernel, (own, left, after(right, res_parts), far_back), (experts, capacity, model))
    res_parts = after(res_parts, total)
    res_far = shifted(res_parts[2], 2)
    res_near = [shifted(part, step) for part, step in zip(res_parts[:2], (3, 1))]
    res_parts = [res_far] + res_near + [res_parts[3]]
    returned = across(total, "ep")
    scaled = call(
        scale_kernel,
        (*res_parts, tokens, coef_weight.reshape(1, model), gate_prob.reshape(1, row_count)),
        (row_count, model + 128),
        dtype=jnp.float32,
    )
    return call(mix_kernel, (route_row, after(returned, scaled), scaled), (row_count, model))


def solution(mesh):
    in_specs = (
        P(("grp", "ep"), None),
        P(("grp", "ep"), None),
        P(("grp", "ep")),
        P(),
        P("ep", None, "grp"),
        P("ep", "grp", None),
        P("ep", "grp"),
        P("grp", "ep"),
    )
    out_specs = P(("grp", "ep"), None)
    return jax.shard_map(local, mesh=mesh, in_specs=in_specs, out_specs=out_specs, check_vma=False)
```

```python
import functools

import jax
import jax.numpy as jnp
from jax import lax
from jax.experimental import pallas as pl
from jax.experimental.pallas import tpu as pltpu
from jax.sharding import PartitionSpec as P

SMEM = pl.BlockSpec(memory_space=pltpu.SMEM)
PARAMS = pltpu.CompilerParams(vmem_limit_bytes=48 * 1024 * 1024)
WHOLE = pltpu.CompilerParams(vmem_limit_bytes=60 * 1024 * 1024)


def cost(rows, model, hidden):
    return pl.CostEstimate(
        flops=4 * rows * model * hidden,
        bytes_accessed=4 * model * (hidden + rows),
        transcendentals=rows * hidden,
    )


def slot_table(route_row, capacity, slots):
    count = route_row.shape[1]
    route = jnp.broadcast_to(route_row, (count, count))
    earlier = lax.broadcasted_iota(jnp.int32, (count, count), 0) < lax.broadcasted_iota(jnp.int32, (count, count), 1)
    place = jnp.sum(jnp.where((route == jnp.transpose(route)) & earlier, 1, 0), axis=0, keepdims=True)
    slot = jnp.broadcast_to(route_row * capacity + place, (slots, count))
    return jnp.where(lax.broadcasted_iota(jnp.int32, (slots, count), 0) == slot, 1.0, 0.0).astype(jnp.bfloat16)


def dispatch_kernel(routes, tokens, out):
    experts, capacity, model = out.shape
    table = slot_table(routes[...], capacity, experts * capacity)
    rows = jnp.dot(table, tokens[...], preferred_element_type=jnp.float32).astype(jnp.bfloat16)
    out[...] = rows.reshape(experts, capacity, model)


def unpack_kernel(slots, out):
    out[...] = slots[...].reshape(out.shape)


def products(rows, weight_in, weight_out, out_dim):
    product = jnp.dot(rows, weight_in, preferred_element_type=jnp.float32)
    hidden = jax.nn.gelu(product, approximate=True).astype(jnp.bfloat16)
    part = lax.dot_general(
        hidden, weight_out, (((1,), (out_dim,)), ((), ())), preferred_element_type=jnp.float32
    )
    return part.astype(jnp.bfloat16)


def expert_kernel(rows, weight_in, weight_out, out):
    out[...] = products(rows[...], weight_in[0], weight_out[0], 0)


def expert_halves_kernel(upper, lower, weight_in, weight_out, out, stack):
    count = upper.shape[0]
    stack[:count, :] = upper[...]
    stack[count:, :] = lower[...]
    out[...] = products(stack[...], weight_in[0], weight_out[0], 0)


def expert_pair_kernel(left, right, weight_in, weight_out, out_left, out_right, stack):
    count = left.shape[0]
    stack[:count, :] = left[...]
    stack[count:, :] = right[...]
    part = products(stack[...], weight_in[0], weight_out[0], 0)
    out_left[...] = part[:count, :]
    out_right[...] = part[count:, :]


def gather_kernel(left, right, far, own, out):
    count = own.shape[0]
    for place, rows in enumerate((left, right, far, own)):
        out[place * count : (place + 1) * count, :] = rows[...]


def residual_kernel(rows, pair, *outs):
    hidden = pair.shape[1] // 2
    part = products(rows[...], pair[:, :hidden], pair[:, hidden:], 1)
    count = part.shape[0] // len(outs)
    for place, out in enumerate(outs):
        out[...] = part[place * count : (place + 1) * count, :]


def sum_kernel(own, left, right, far, out):
    total = own[...].astype(jnp.float32) + left[...].astype(jnp.float32)
    total = total + right[...].astype(jnp.float32) + far[...].astype(jnp.float32)
    out[...] = total.astype(jnp.bfloat16).reshape(out.shape)


def scale_kernel(far, left, right, own, tokens, weight, gate, out):
    model = own.shape[1]
    res = left[...].astype(jnp.float32) + right[...].astype(jnp.float32)
    res = res + far[...].astype(jnp.float32) + own[...].astype(jnp.float32)
    logit = jnp.sum(tokens[...].astype(jnp.float32) * weight[...].astype(jnp.float32), axis=1, keepdims=True)
    coef = 1.0 / (1.0 + jnp.exp(-logit))
    gates = jnp.transpose(jnp.broadcast_to(gate[...], (128, gate.shape[1])))
    out[:, :model] = coef * res
    out[:, model:] = (1.0 - coef) * gates


def mix_kernel(routes, slots, scaled, out):
    experts, capacity, model = slots.shape
    table = slot_table(routes[...], capacity, experts * capacity)
    rows = slots[...].reshape(experts * capacity, model)
    expert_out = lax.dot_general(table, rows, (((0,), (0,)), ((), ())), preferred_element_type=jnp.float32)
    out[...] = (scaled[:, :model] + scaled[:, model : model + 1] * expert_out).astype(jnp.bfloat16)


def block(shape):
    return pl.BlockSpec(shape, lambda i: (0,) * len(shape))


def call(kernel, ins, shape, estimate=None, scratch=(), count=1, params=PARAMS, dtype=jnp.bfloat16):
    whole = jax.ShapeDtypeStruct(shape, dtype)
    return pl.pallas_call(
        kernel,
        grid=(1,),
        in_specs=[SMEM if value.ndim == 1 else block(value.shape) for value in ins],
        out_specs=block(shape) if count == 1 else [block(shape)] * count,
        out_shape=whole if count == 1 else [whole] * count,
        scratch_shapes=scratch,
        compiler_params=params,
        cost_estimate=estimate,
    )(*ins)


def shifted(value, step):
    size = lax.axis_size("grp")
    return lax.ppermute(value, "grp", [(i, (i + step) % size) for i in range(size)])


def across(value, axis):
    return lax.all_to_all(value, axis, split_axis=0, concat_axis=0, tiled=True)


def after(value, earlier):
    return lax.optimization_barrier((value, earlier))[0]


def local(tokens, routes, gate_prob, coef_weight, exp_up, exp_down, res_up, res_down):
    row_count, model = tokens.shape
    groups, experts = lax.axis_size("grp"), lax.axis_size("ep")
    capacity = 2 * row_count // experts
    slots = experts * capacity
    hidden = exp_up.shape[2]
    route_row = routes.reshape(1, row_count)

    res_pair = jnp.concatenate([res_up, res_down.T], axis=1)
    res_all = lax.all_gather(res_pair, "ep", axis=0, tiled=True)

    outgoing = call(dispatch_kernel, (route_row, tokens), (experts, capacity, model), params=WHOLE)
    arrived = across(outgoing, "ep")
    other_tokens = [shifted(tokens, step) for step in (1, 3, 2)]
    arrived = after(arrived, other_tokens)
    arrived = call(unpack_kernel, (arrived,), (slots, model))
    left, right = shifted(arrived, 1), shifted(arrived, 3)
    half, shape, weights = slots // 2, arrived.shape, (exp_up, exp_down)
    whole_rows = call(gather_kernel, (*other_tokens, tokens), (groups * row_count, model))
    own = call(expert_kernel, (after(arrived, whole_rows), *weights), shape, cost(slots, model, hidden))
    left, right = after((left, right), own)
    upper, lower = shifted(left[:half], 1), shifted(right[half:], 3)
    near_left, near_right = call(
        expert_pair_kernel,
        (left, right, *weights),
        shape,
        cost(2 * slots, model, hidden),
        scratch=[pltpu.VMEM((2 * slots, model), jnp.bfloat16)],
        count=2,
    )
    far = call(
        expert_halves_kernel,
        (after(upper, near_left), lower, *weights),
        shape,
        cost(slots, model, hidden),
        scratch=[pltpu.VMEM(shape, jnp.bfloat16)],
    )
    left, right, far_back = shifted(near_left, 3), shifted(near_right, 1), shifted(far, 2)

    res_parts = call(
        residual_kernel,
        (after(whole_rows, far), res_all),
        (row_count, model),
        cost(groups * row_count, model, hidden),
        count=groups,
        params=WHOLE,
    )
    row_block = pl.BlockSpec((slots // 2, model), lambda i: (i, 0))
    total = pl.pallas_call(
        sum_kernel,
        grid=(2,),
        in_specs=[row_block] * 4,
        out_specs=pl.BlockSpec((experts // 2, capacity, model), lambda i: (i, 0, 0)),
        out_shape=jax.ShapeDtypeStruct((experts, capacity, model), jnp.bfloat16),
        compiler_params=PARAMS,
    )(own, left, after(right, res_parts), far_back)
    res_parts = after(res_parts, total)
    res_far = shifted(res_parts[2], 2)
    res_near = [shifted(part, step) for part, step in zip(res_parts[:2], (3, 1))]
    res_parts = [res_far] + res_near + [res_parts[3]]
    returned = across(total, "ep")
    scaled = call(
        scale_kernel,
        (*res_parts, tokens, coef_weight.reshape(1, model), gate_prob.reshape(1, row_count)),
        (row_count, model + 128),
        dtype=jnp.float32,
    )
    return call(mix_kernel, (route_row, after(returned, scaled), scaled), (row_count, model))


def solution(mesh):
    in_specs = (
        P(("grp", "ep"), None),
        P(("grp", "ep"), None),
        P(("grp", "ep")),
        P(),
        P("ep", None, "grp"),
        P("ep", "grp", None),
        P("ep", "grp"),
        P("grp", "ep"),
    )
    out_specs = P(("grp", "ep"), None)
    return jax.shard_map(local, mesh=mesh, in_specs=in_specs, out_specs=out_specs, check_vma=False)
```
